32 devices in a mesh: groups: 2 (over y), src: 4 (over z), dst: 4 (over x, core).
Axes of the slice: x: 2, y: 2, z: 4, core: 2. Of those that a mesh axis runs over, the one named last changes fastest.
Arguments:
- source_table: float32 [16384, 400], P(('groups', 'src', 'dst')), parts along dimension 0
- source_state: float32 [16384], P(('groups', 'src', 'dst')), parts along dimension 0, may hold values from 0.01 to 0.5
- target_table: float32 [16384, 400], P(('groups', 'src', 'dst')), parts along dimension 0
- target_state: float32 [16384], P(('groups', 'src', 'dst')), parts along dimension 0, may hold values from 0.01 to 0.5
- relation_table: float32 [2560, 400], P('groups'), parts along dimension 0, may hold values from -6 to 6
- relation_state: float32 [2560], P('groups'), parts along dimension 0, may hold values from 0.01 to 0.5
- edge_list: int32 [3, 65536], P(None, ('groups', 'src', 'dst')), parts along dimension 1, may hold values from 0 to 1279, as said below
- edge_count: int32 [32], P(('groups', 'src', 'dst')), parts along dimension 0, may hold values from 1 to 2048, 10922 in all
- negative_ids: int32 [128, 512], P(('groups', 'src', 'dst')), parts along dimension 0, may hold values from 0 to 127
- source_lists: int32 [128, 64], P(('groups', 'src', 'dst')), parts along dimension 0, may hold values from 0 to 511
- target_lists: int32 [128, 32], P(('groups', 'src', 'dst')), parts along dimension 0, may hold values from 0 to 511
Outputs:
- new_source_table: float32 [16384, 400], P(('groups', 'src', 'dst')), parts along dimension 0
- new_source_state: float32 [16384], P(('groups', 'src', 'dst')), parts along dimension 0
- new_target_table: float32 [16384, 400], P(('groups', 'src', 'dst')), parts along dimension 0
- new_target_state: float32 [16384], P(('groups', 'src', 'dst')), parts along dimension 0
- new_relation_table: float32 [2560, 400], P('groups'), parts along dimension 0
- new_relation_state: float32 [2560], P('groups'), parts along dimension 0
The draws below stay inside these ranges and needn't reach their ends.
There are 2 independent parts, one for each index of `groups`. The reference program is written for one: setup_inputs(seed, part) draws one part's arguments, and reference() takes and returns one part's arrays. A program takes and returns all parts, laid end to end along the dimension named above; each array names one. Nothing has to cross between parts.
Inputs may be any that keep to these rules, and one draw needn't show every extreme that they name: `edge_list`: row 0 is a slot among a bucket's 4 * 64 source slots, row 1 a relation, row 2 a slot among its 128 destination slots. Only the first edge_count edges of a bucket are live. `edge_count`: some bucket is full in every draw; every count is at least one. `negative_ids`: slots among a bucket's destination slots; repeats allowed. `source_lists`: local row numbers of the owner; repeats allowed. `target_lists`: local row numbers of the owner; repeats allowed.
All inputs are finite; a program needn't handle non-finite values. No bound on the sum of `edge_count` on one device may be relied on, other than what follows from the above.
Results may differ from the reference program's by a relative error of at most 0.0028.
Values may be sent and summed in bfloat16 or wider, within the bound.
A program may use at most 64 MiB of HBM per device.

```python
import math
import jax
import jax.numpy as jnp
import numpy as np
from jax import lax

D = 400
REL = 1280
OWN = 512
CAP_S = 64
CAP_D = 32
SPAN = 512
NEG = 512
SPANS = 4
EDGE_CAP = 2048
EDGES = 32768
ENT = 8192
N_SRC = 4
N_DST = 4


def scaled_table(key, base_values):
    row_key, column_key = jax.random.split(key)
    row_scale = jnp.exp(jax.random.uniform(row_key, (base_values.shape[0], 1), jnp.float32, math.log(0.3), math.log(3.0)))
    column_scale = jnp.exp(jax.random.uniform(column_key, (1, base_values.shape[1]), jnp.float32, math.log(0.5), math.log(2.0)))
    return 0.2 * base_values * row_scale * column_scale


def draw_source_table(key, part):
    key = jax.random.fold_in(key, 21)
    base_key, scale_key = jax.random.split(key)
    base_values = jax.random.normal(base_key, (ENT, D), jnp.float32)
    return scaled_table(scale_key, base_values)


def draw_target_table(key, part):
    key = jax.random.fold_in(key, 29)
    base_key, scale_key = jax.random.split(key)
    base_values = jax.random.normal(base_key, (ENT, D), jnp.float32)
    return scaled_table(scale_key, base_values)


def draw_edge_list(key, part):
    key = jax.random.fold_in(key, 37)
    subkeys = jax.random.split(key, 5)
    source_slot = jax.random.randint(subkeys[0], (EDGES,), 0, N_DST * CAP_S)
    target_slot = jax.random.randint(subkeys[1], (EDGES,), 0, N_SRC * CAP_D)
    home_count = max(REL // (N_SRC * N_DST), 1)
    bucket = jnp.arange(EDGES, dtype=jnp.int32) // EDGE_CAP
    nearby = (bucket * home_count + jax.random.randint(subkeys[2], (EDGES,), 0, home_count)) % REL
    spread = jax.random.randint(subkeys[3], (EDGES,), 0, REL)
    choose_home = jax.random.randint(subkeys[4], (EDGES,), 0, 2)
    relation = jnp.where(choose_home == 1, nearby, spread)
    return jnp.stack([source_slot, relation, target_slot]).astype(jnp.int32)


def touch_ends(drawn, key, smallest, largest):
    spot = [jax.random.randint(jax.random.fold_in(key, axis), (), 0, length) for axis, length in enumerate(drawn.shape)]
    widest = drawn.shape.index(max(drawn.shape))
    beside = spot[:widest] + [(spot[widest] + 1) % drawn.shape[widest]] + spot[widest + 1:]
    return drawn.at[tuple(spot)].set(smallest).at[tuple(beside)].set(largest)


def block_levels(stream_key, shape, pieces, low, high):
    factor_of = 1.0
    for dim, parts in pieces:
        steps = jax.random.uniform(jax.random.fold_in(jax.random.fold_in(stream_key, 6), dim), (parts,), jnp.float32, low / len(pieces), high / len(pieces))
        factor_of = factor_of * jnp.repeat(jnp.exp(steps), shape[dim] // parts).reshape((-1,) + (1,) * (len(shape) - 1 - dim))
    return factor_of


def profile(number_of, total, bound, slope):
    loads = [(1 << 20) // math.isqrt(grade ** slope) + 1 for grade in range(2, number_of + 1)]
    spare, counts = total - bound - (number_of - 1), [1] * (number_of - 1)
    while spare > 0:
        movable = [i for i in range(number_of - 1) if counts[i] < bound]
        pool, left = sum([loads[i] for i in movable]), spare
        for i in movable:
            more = min(bound - counts[i], max(1, left * loads[i] // pool), spare)
            counts[i] = counts[i] + more
            spare = spare - more
    return np.array([bound] + counts)


def uneven_parts(stream_key, count, total, limit, slope):
    if count == 2:
        one = jax.random.randint(stream_key, (), max(1, total - limit), min(limit, total - 1) + 1)
        return jnp.stack([one, total - one])
    sizes = jnp.asarray(profile(count, total, limit, slope), jnp.int32)
    pairs = (count - 1) // 2
    donor, receiver = sizes[1:1 + 2 * pairs:2], sizes[2:2 + 2 * pairs:2]
    slack = jnp.minimum(donor - 1, limit - receiver)
    shifted = jax.random.randint(jax.random.fold_in(stream_key, 1), (pairs,), 0, 1 << 20) % (slack + 1)
    sizes = sizes.at[1:1 + 2 * pairs:2].set(donor - shifted).at[2:2 + 2 * pairs:2].set(receiver + shifted)
    return sizes[jax.random.permutation(jax.random.fold_in(stream_key, 2), count)]


def normal_values(key, shape, scale, limit, kind=jnp.bfloat16):
    drawn = scale * jax.random.normal(key, shape, jnp.float32)
    return jnp.clip(drawn, min=-limit, max=limit).astype(kind)


def setup_inputs(seed: int = 0, part: int = 0) -> dict:
    seeds = jax.random.split(jax.random.key(seed), 12)
    part_keys = jax.random.split(jax.random.fold_in(seeds[11], part), 12)
    return {
        "source_table": draw_source_table(jax.random.fold_in(jax.random.fold_in(seeds[11], part), 71), part),
        "source_state": jnp.clip(jnp.exp(math.log(0.5) - 3.912023 * jax.random.uniform(part_keys[1], (ENT,), jnp.float32) ** block_levels(part_keys[1], (ENT,), ((0, 16),), -0.2, 0.2)), 0.01, 0.5),
        "target_table": draw_target_table(jax.random.fold_in(jax.random.fold_in(seeds[11], part), 71), part),
        "target_state": jnp.clip(jnp.exp(math.log(0.5) - 3.912023 * jax.random.uniform(part_keys[3], (ENT,), jnp.float32) ** block_levels(part_keys[3], (ENT,), ((0, 16),), -0.2, 0.2)), 0.01, 0.5),
        "relation_table": normal_values(part_keys[4], (REL, D), 1.0, 6.0, jnp.float32),
        "relation_state": jnp.clip(jnp.exp(jax.random.uniform(part_keys[5], (REL,), jnp.float32, math.log(0.01), math.log(0.5))), 0.01, 0.5),
        "edge_list": draw_edge_list(jax.random.fold_in(jax.random.fold_in(seeds[11], part), 71), part),
        "edge_count": uneven_parts(part_keys[7], N_SRC * N_DST, EDGE_CAP * N_SRC * N_DST // 3, EDGE_CAP, 2).astype(jnp.int32),
        "negative_ids": touch_ends(jax.random.randint(part_keys[8], (N_SRC * N_DST * SPANS, NEG), 0, N_SRC * CAP_D), jax.random.fold_in(part_keys[8], 1), 0, (N_SRC * CAP_D) - 1).astype(jnp.int32),
        "source_lists": touch_ends(jax.random.randint(part_keys[9], (N_SRC * N_DST * N_DST, CAP_S), 0, OWN), jax.random.fold_in(part_keys[9], 1), 0, OWN - 1).astype(jnp.int32),
        "target_lists": touch_ends(jax.random.randint(part_keys[10], (N_SRC * N_DST * N_SRC, CAP_D), 0, OWN), jax.random.fold_in(part_keys[10], 1), 0, OWN - 1).astype(jnp.int32),
    }


learn_rate = 0.1

def complex_product(first_factor, second_factor):
    half_width = first_factor.shape[-1] // 2
    first_real = first_factor[..., :half_width]
    first_imag = first_factor[..., half_width:]
    second_real = second_factor[..., :half_width]
    second_imag = second_factor[..., half_width:]
    return jnp.concatenate([first_real * second_real - first_imag * second_imag, first_real * second_imag + first_imag * second_real], axis=-1)

def conjugate(values):
    half_width = values.shape[-1] // 2
    return jnp.concatenate([values[..., :half_width], -values[..., half_width:]], axis=-1)

def block_terms(source, relation, target, negatives, alive_mask):
    query_row = complex_product(source, relation)
    query_low = query_row.astype(jnp.bfloat16)
    positive = lax.optimization_barrier(jnp.sum(query_row * target, axis=1))
    negative = jnp.dot(query_low, negatives.T, preferred_element_type=jnp.float32)
    pos_weight = -alive_mask * jax.nn.sigmoid(-positive)
    neg_weight = (jax.nn.sigmoid(negative) * (alive_mask[:, None] / negatives.shape[0])).astype(jnp.bfloat16)
    query_grad = pos_weight[:, None] * target + jnp.dot(neg_weight, negatives, preferred_element_type=jnp.float32)
    target_grad = pos_weight[:, None] * query_row
    negative_grad = jnp.dot(neg_weight.T, query_low, preferred_element_type=jnp.float32)
    source_grad = complex_product(query_grad, conjugate(relation))
    relation_grad = complex_product(query_grad, conjugate(source))
    return (source_grad, target_grad, negative_grad, relation_grad)

def bucket_terms(src_rows, dst_rows, relation_table, bucket_edges, live_count, bucket_negs):
    row_width = src_rows.shape[1]

    def one_block(carried, block_index):
        source_acc, target_acc, relation_acc = carried
        block_edges = lax.dynamic_slice_in_dim(bucket_edges, block_index * SPAN, SPAN, 1)
        position = block_index * SPAN + jnp.arange(SPAN, dtype=jnp.int32)
        alive_mask = (position < live_count).astype(jnp.float32)
        source = src_rows[block_edges[0]].astype(jnp.float32)
        relation = relation_table[block_edges[1]]
        target = dst_rows[block_edges[2]].astype(jnp.float32)
        negative_slots = bucket_negs[block_index]
        negatives = dst_rows[negative_slots]
        source_grad, target_grad, negative_grad, relation_grad = block_terms(source, relation, target, negatives, alive_mask)
        source_acc = source_acc.at[block_edges[0]].add(source_grad)
        target_acc = target_acc.at[block_edges[2]].add(target_grad).at[negative_slots].add(negative_grad)
        relation_acc = relation_acc.at[block_edges[1]].add(relation_grad)
        return ((source_acc, target_acc, relation_acc), None)
    initial = (jnp.zeros((src_rows.shape[0], row_width), jnp.float32), jnp.zeros((dst_rows.shape[0], row_width), jnp.float32), jnp.zeros(relation_table.shape, jnp.float32))
    carried, _ = lax.scan(one_block, initial, jnp.arange(SPANS, dtype=jnp.int32))
    return carried

def row_update(table, state, grad):
    new_state = state + lax.optimization_barrier(jnp.mean(grad * grad, axis=1))
    return (table - learn_rate * grad / jnp.sqrt(new_state)[:, None], new_state)

def reference(source_table, source_state, target_table, target_state, relation_table, relation_state, edge_list, edge_count, negative_ids, source_lists, target_lists):
    source_grid = source_lists.reshape(N_SRC, N_DST, N_DST, CAP_S)
    target_grid = target_lists.reshape(N_SRC, N_DST, N_SRC, CAP_D)
    owners_row = jnp.arange(N_DST, dtype=jnp.int32)
    owners_column = jnp.arange(N_SRC, dtype=jnp.int32)

    def one_bucket(carried, bucket):
        source_total, target_total, relation_total = carried
        grid_row = bucket // N_DST
        grid_column = bucket % N_DST
        source_ids = ((grid_row * N_DST + owners_row)[:, None] * OWN + source_grid[grid_row, :, grid_column, :]).reshape(-1).astype(jnp.int32)
        target_ids = ((owners_column * N_DST + grid_column)[:, None] * OWN + target_grid[:, grid_column, grid_row, :]).reshape(-1).astype(jnp.int32)
        src_rows = source_table[source_ids].astype(jnp.bfloat16)
        dst_rows = target_table[target_ids].astype(jnp.bfloat16)
        bucket_edges = lax.dynamic_slice_in_dim(edge_list, bucket * EDGE_CAP, EDGE_CAP, 1)
        bucket_negs = lax.dynamic_slice_in_dim(negative_ids, bucket * SPANS, SPANS, 0)
        source_grad, target_grad, relation_grad = bucket_terms(src_rows, dst_rows, relation_table, bucket_edges, edge_count[bucket], bucket_negs)
        return ((source_total.at[source_ids].add(source_grad), target_total.at[target_ids].add(target_grad), relation_total + relation_grad), None)
    initial = (jnp.zeros((ENT, D), jnp.float32), jnp.zeros((ENT, D), jnp.float32), jnp.zeros((REL, D), jnp.float32))
    totals, _ = lax.scan(one_bucket, initial, jnp.arange(N_SRC * N_DST, dtype=jnp.int32))
    source_sum, target_sum, relation_total = totals
    new_source_table, new_source_state = row_update(source_table, source_state, source_sum)
    new_target_table, new_target_state = row_update(target_table, target_state, target_sum)
    new_relation_table, new_relation_state = row_update(relation_table, relation_state, relation_total)
    return (new_source_table, new_source_state, new_target_table, new_target_state, new_relation_table, new_relation_state)
```

```python
import functools

import jax
import jax.numpy as jnp
from jax import lax
from jax.experimental import pallas as pl
from jax.experimental.pallas import tpu as pltpu
from jax.sharding import PartitionSpec as P

learn_rate = 0.1
MESH = pl.DeviceIdType.MESH
BF = jnp.bfloat16
F32 = jnp.float32


def dot(a, b):
    return jnp.dot(a, b, preferred_element_type=F32)


def dot_nt(a, b):
    return lax.dot_general(a, b, (((1,), (1,)), ((), ())), preferred_element_type=F32)


def dot_tn(a, b):
    return lax.dot_general(a, b, (((0,), (0,)), ((), ())), preferred_element_type=F32)


def one_hot(rows, ids):
    where = lax.broadcasted_iota(jnp.int32, (rows, ids.shape[1]), 0) == ids
    return jnp.where(where, 1.0, 0.0).astype(BF)


def greet(n_src, n_dst, me_s, me_d):
    barrier = pltpu.get_barrier_semaphore()
    for k in range(1, n_dst):
        pl.semaphore_signal(
            barrier, 1, device_id={"dst": lax.rem(me_d + k, n_dst)}, device_id_type=MESH
        )
    for k in range(1, n_src):
        pl.semaphore_signal(
            barrier, 1, device_id={"src": lax.rem(me_s + k, n_src)}, device_id_type=MESH
        )
    pl.semaphore_wait(barrier, n_src + n_dst - 2)


def swap(axis, n, me, cap, out_ref, in_ref, send, recv):
    copies = []
    for k in range(1, n):
        peer = lax.rem(me + k, n)
        copy = pltpu.make_async_remote_copy(
            src_ref=out_ref.at[pl.ds(pl.multiple_of(peer * cap, cap), cap)],
            dst_ref=in_ref.at[pl.ds(pl.multiple_of(me * cap, cap), cap)],
            send_sem=send.at[k - 1],
            recv_sem=recv.at[k - 1],
            device_id={axis: peer},
            device_id_type=MESH,
        )
        copy.start()
        copies.append(copy)
    return copies


def fetch_kernel(
    n_src, n_dst, stab, ttab, slist, tlist, srows, drows, sout, tout, sin, tin, s1, r1, s2, r2
):
    me_s = lax.axis_index("src")
    me_d = lax.axis_index("dst")
    cs = slist.shape[1]
    cd = tlist.shape[1]
    greet(n_src, n_dst, me_s, me_d)
    table = stab[...].astype(BF)
    for p in range(n_dst):
        sout[p * cs : (p + 1) * cs, :] = dot_tn(
            one_hot(table.shape[0], slist[p : p + 1, :]), table
        ).astype(BF)
    first = swap("dst", n_dst, me_d, cs, sout, sin, s1, r1)
    table = ttab[...].astype(BF)
    for p in range(n_src):
        tout[p * cd : (p + 1) * cd, :] = dot_tn(
            one_hot(table.shape[0], tlist[p : p + 1, :]), table
        ).astype(BF)
    second = swap("src", n_src, me_s, cd, tout, tin, s2, r2)
    mine = pl.ds(pl.multiple_of(me_d * cs, cs), cs)
    sin[mine, :] = sout[mine, :]
    mine = pl.ds(pl.multiple_of(me_s * cd, cd), cd)
    tin[mine, :] = tout[mine, :]
    for copy in first:
        copy.wait()
    srows[...] = sin[...]
    for copy in second:
        copy.wait()
    drows[...] = tin[...]


def bucket_kernel(
    srows, drows, rel, edges, count, negs, sgrad, tgrad, rgrad, rel_hi, rel_lo, src_t, dst_t, hots, rg
):
    slots = srows.shape[0]
    targets = drows.shape[0]
    relations, width = rel.shape
    half = width // 2
    blocks, negatives = negs.shape
    span = edges.shape[1] // blocks
    table = rel[...]
    high = table.astype(BF)
    rel_hi[...] = high.T
    rel_lo[...] = (table - high.astype(F32)).astype(BF).T
    src_t[...] = srows[...].T
    dst_t[...] = drows[...].T
    source_acc = jnp.zeros((slots, width), F32)
    target_acc = jnp.zeros((targets, width), F32)
    live = count[0]
    for c in range(blocks):
        cols = slice(c * span, (c + 1) * span)
        uses = one_hot(targets, negs[c : c + 1, :])
        uses = jnp.sum(uses.astype(F32), axis=1, keepdims=True)
        hot_s = one_hot(slots, edges[0:1, cols])
        hot_r = one_hot(relations, edges[1:2, cols])
        hots[:, cols] = hot_r
        is_target = (
            lax.broadcasted_iota(jnp.int32, (targets, span), 0) == edges[2:3, cols]
        )
        place = c * span + lax.broadcasted_iota(jnp.int32, (1, span), 1)
        alive = jnp.where(place < live, 1.0, 0.0)
        source = dot(src_t[...], hot_s)
        relation = dot(rel_hi[...], hot_r) + dot(rel_lo[...], hot_r)
        sr, si = source[:half], source[half:]
        rr, ri = relation[:half], relation[half:]
        query = jnp.concatenate([sr * rr - si * ri, sr * ri + si * rr], axis=0)
        low = query.astype(BF)
        rest = (query - low.astype(F32)).astype(BF)
        logits = dot(drows[...], low)
        extra = dot(drows[...], rest)
        positive = jnp.sum(jnp.where(is_target, logits + extra, 0.0), axis=0, keepdims=True)
        pos_weight = -alive * jax.nn.sigmoid(-positive)
        neg_weight = (jax.nn.sigmoid(logits) * (alive / negatives)).astype(BF).astype(F32)
        weight = jnp.where(is_target, pos_weight, 0.0) + uses * neg_weight
        w_high = weight.astype(BF)
        w_rest = (weight - w_high.astype(F32)).astype(BF)
        grad = dot(dst_t[...], w_high) + dot(dst_t[...], w_rest)
        target_acc = target_acc + (
            dot_nt(w_high, low) + (dot_nt(w_rest, low) + dot_nt(w_high, rest))
        )
        gr, gi = grad[:half], grad[half:]
        source_grad = jnp.concatenate([gr * rr + gi * ri, gi * rr - gr * ri], axis=0)
        source_acc = source_acc + dot_nt(hot_s, source_grad.astype(BF))
        rg[:, cols] = jnp.concatenate(
            [gr * sr + gi * si, gi * sr - gr * si], axis=0
        ).astype(BF)
    sgrad[...] = source_acc.astype(BF)
    tgrad[...] = target_acc.astype(BF)
    rgrad[0:relations, :] = dot_nt(hots[...], rg[...]).astype(BF)
    if rgrad.shape[0] > relations:
        rgrad[relations:, :] = jnp.zeros((rgrad.shape[0] - relations, width), BF)


def return_kernel(
    n_src, n_dst, pieces, step,
    sgrad, tgrad, rgrad, slist, tlist,
    ssum, tsum, total,
    sin, tin, core_in, x_in, z_in, core_sum, x_sum, full,
    s1, r1, s2, r2, cs_s, cs_r, xs_s, xs_r, zs_s, zs_r, zg_s, zg_r, xg_s, xg_r, cg_s, cg_r,
):
    me_s = lax.axis_index("src")
    me_d = lax.axis_index("dst")
    core = lax.rem(me_d, 2)
    chip = me_d // 2
    chips = n_dst // 2
    cs = slist.shape[1]
    cd = tlist.shape[1]
    z_rows = step
    x_rows = z_rows * n_src
    c_rows = x_rows * chips
    p_rows = c_rows * 2

    def rows(start, count):
        return pl.ds(pl.multiple_of(start, 16), count)

    def push(src, dst, send, recv, axis, peer):
        copy = pltpu.make_async_remote_copy(
            src_ref=src, dst_ref=dst, send_sem=send, recv_sem=recv,
            device_id={axis: peer}, device_id_type=MESH,
        )
        copy.start()
        return copy

    greet(n_src, n_dst, me_s, me_d)
    other = me_d + 1 - 2 * core
    started = {}
    for p in range(pieces):
        started["c", p] = [
            push(
                rgrad.at[rows(p * p_rows + (1 - core) * c_rows, c_rows)],
                core_in.at[pl.ds(p * c_rows, c_rows)],
                cs_s.at[p], cs_r.at[p], "dst", other,
            )
        ]
    first = swap("dst", n_dst, me_d, cs, sgrad, sin, s1, r1)
    second = swap("src", n_src, me_s, cd, tgrad, tin, s2, r2)
    mine = pl.ds(pl.multiple_of(me_d * cs, cs), cs)
    sin[mine, :] = sgrad[mine, :]
    mine = pl.ds(pl.multiple_of(me_s * cd, cd), cd)
    tin[mine, :] = tgrad[mine, :]

    def stage_x(p):
        for copy in started["c", p]:
            copy.wait()
        here = pl.ds(p * c_rows, c_rows)
        own = rgrad[rows(p * p_rows + core * c_rows, c_rows), :]
        core_sum[here, :] = (own.astype(F32) + core_in[here, :].astype(F32)).astype(BF)
        started["x", p] = []
        for k in range(1, chips):
            peer = lax.rem(chip + k, chips)
            slot = p * (chips - 1) + k - 1
            started["x", p].append(
                push(
                    core_sum.at[rows(p * c_rows + peer * x_rows, x_rows)],
                    x_in.at[pl.ds(slot * x_rows, x_rows)],
                    xs_s.at[slot], xs_r.at[slot], "dst", peer * 2 + core,
                )
            )

    def stage_z(p):
        for copy in started["x", p]:
            copy.wait()
        value = core_sum[rows(p * c_rows + chip * x_rows, x_rows), :].astype(F32)
        for k in range(1, chips):
            slot = p * (chips - 1) + k - 1
            value = value + x_in[pl.ds(slot * x_rows, x_rows), :].astype(F32)
        x_sum[pl.ds(p * x_rows, x_rows), :] = value.astype(BF)
        started["z", p] = []
        for k in range(1, n_src):
            peer = lax.rem(me_s + k, n_src)
            slot = p * (n_src - 1) + k - 1
            started["z", p].append(
                push(
                    x_sum.at[rows(p * x_rows + peer * z_rows, z_rows)],
                    z_in.at[pl.ds(slot * z_rows, z_rows)],
                    zs_s.at[slot], zs_r.at[slot], "src", peer,
                )
            )

    def place(p, chip_at, src_at):
        return p * p_rows + core * c_rows + chip_at * x_rows + src_at * z_rows

    def gather_z(p):
        for copy in started["z", p]:
            copy.wait()
        value = x_sum[rows(p * x_rows + me_s * z_rows, z_rows), :].astype(F32)
        for k in range(1, n_src):
            slot = p * (n_src - 1) + k - 1
            value = value + z_in[pl.ds(slot * z_rows, z_rows), :].astype(F32)
        here = rows(place(p, chip, me_s), z_rows)
        full[here, :] = value.astype(BF)
        started["gz", p] = []
        for k in range(1, n_src):
            peer = lax.rem(me_s + k, n_src)
            slot = p * (n_src - 1) + k - 1
            started["gz", p].append(
                push(full.at[here], full.at[here], zg_s.at[slot], zg_r.at[slot], "src", peer)
            )

    def gather_x(p):
        for copy in started["gz", p]:
            copy.wait()
        here = rows(place(p, chip, 0), x_rows)
        started["gx", p] = []
        for k in range(1, chips):
            peer = lax.rem(chip + k, chips)
            slot = p * (chips - 1) + k - 1
            started["gx", p].append(
                push(
                    full.at[here], full.at[here], xg_s.at[slot], xg_r.at[slot],
                    "dst", peer * 2 + core,
                )
            )

    def gather_core(p):
        for copy in started["gx", p]:
            copy.wait()
        here = rows(place(p, 0, 0), c_rows)
        started["gc", p] = [
            push(full.at[here], full.at[here], cg_s.at[p], cg_r.at[p], "dst", other)
        ]

    def sums():
        for copy in first:
            copy.wait()
        value = jnp.zeros(ssum.shape, F32)
        for p in range(n_dst):
            value = value + dot(
                one_hot(ssum.shape[0], slist[p : p + 1, :]), sin[p * cs : (p + 1) * cs, :]
            )
        ssum[...] = value
        for copy in second:
            copy.wait()
        value = jnp.zeros(tsum.shape, F32)
        for p in range(n_src):
            value = value + dot(
                one_hot(tsum.shape[0], tlist[p : p + 1, :]), tin[p * cd : (p + 1) * cd, :]
            )
        tsum[...] = value

    stages = [stage_x, stage_z, gather_z, gather_x, gather_core]
    for t in range(pieces + len(stages) - 1):
        for s in reversed(range(len(stages))):
            if 0 <= t - s < pieces:
                stages[s](t - s)
        if t == pieces - 1:
            sums()
    for p in range(pieces):
        for copy in started["gc", p]:
            copy.wait()
    total[...] = full[0 : total.shape[0], :]


def update_rows(table, state, grad):
    new_state = state + jnp.mean(grad * grad, axis=1)
    return (table - learn_rate * grad / jnp.sqrt(new_state)[:, None], new_state)


VM = pl.BlockSpec(memory_space=pltpu.VMEM)
SM = pl.BlockSpec(memory_space=pltpu.SMEM)
LIMIT = 48 * 1024 * 1024


def body(
    source_table, source_state, target_table, target_state, relation_table, relation_state,
    edge_list, edge_count, negative_ids, source_lists, target_lists,
):
    n_dst = lax.axis_size("dst")
    n_src = lax.axis_size("src")
    width = source_table.shape[1]
    cs = source_lists.shape[1]
    cd = target_lists.shape[1]
    own = source_table.shape[0]
    relations = relation_table.shape[0]
    group = n_src * n_dst
    share = -(-relations // (group * 16)) * 16
    step = 16
    pieces = share // step
    padded = share * group
    slots, targets = n_dst * cs, n_src * cd
    dma = pltpu.SemaphoreType.DMA

    src_rows, dst_rows = pl.pallas_call(
        functools.partial(fetch_kernel, n_src, n_dst),
        out_shape=[
            jax.ShapeDtypeStruct((slots, width), BF),
            jax.ShapeDtypeStruct((targets, width), BF),
        ],
        in_specs=[VM] * 4,
        out_specs=[VM] * 2,
        scratch_shapes=[
            pltpu.VMEM((slots, width), BF),
            pltpu.VMEM((targets, width), BF),
            pltpu.VMEM((slots, width), BF),
            pltpu.VMEM((targets, width), BF),
            dma((n_dst - 1,)), dma((n_dst - 1,)), dma((n_src - 1,)), dma((n_src - 1,)),
        ],
        compiler_params=pltpu.CompilerParams(
            collective_id=0, has_side_effects=True, vmem_limit_bytes=LIMIT
        ),
        name="fetch",
    )(source_table, target_table, source_lists, target_lists)

    edges = edge_list.shape[1]
    sgrad, tgrad, rgrad = pl.pallas_call(
        bucket_kernel,
        out_shape=[
            jax.ShapeDtypeStruct((slots, width), BF),
            jax.ShapeDtypeStruct((targets, width), BF),
            jax.ShapeDtypeStruct((padded, width), BF),
        ],
        in_specs=[VM, VM, VM, VM, SM, VM],
        out_specs=[VM] * 3,
        scratch_shapes=[
            pltpu.VMEM((width, relations), BF),
            pltpu.VMEM((width, relations), BF),
            pltpu.VMEM((width, slots), BF),
            pltpu.VMEM((width, targets), BF),
            pltpu.VMEM((relations, edges), BF),
            pltpu.VMEM((width, edges), BF),
        ],
        compiler_params=pltpu.CompilerParams(vmem_limit_bytes=LIMIT),
        name="bucket",
    )(src_rows, dst_rows, relation_table, edge_list, edge_count, negative_ids)

    chips = n_dst // 2
    x_rows = step * n_src
    c_rows = x_rows * chips
    core_n = pieces
    x_n = pieces * (chips - 1)
    z_n = pieces * (n_src - 1)
    source_sum, target_sum, relation_total = pl.pallas_call(
        functools.partial(return_kernel, n_src, n_dst, pieces, step),
        out_shape=[
            jax.ShapeDtypeStruct((own, width), F32),
            jax.ShapeDtypeStruct((target_table.shape[0], width), F32),
            jax.ShapeDtypeStruct((relations, width), BF),
        ],
        in_specs=[VM] * 5,
        out_specs=[VM] * 3,
        scratch_shapes=[
            pltpu.VMEM((slots, width), BF),
            pltpu.VMEM((targets, width), BF),
            pltpu.VMEM((pieces * c_rows, width), BF),
            pltpu.VMEM((x_n * x_rows, width), BF),
            pltpu.VMEM((z_n * step, width), BF),
            pltpu.VMEM((pieces * c_rows, width), BF),
            pltpu.VMEM((pieces * x_rows, width), BF),
            pltpu.VMEM((padded, width), BF),
            dma((n_dst - 1,)), dma((n_dst - 1,)), dma((n_src - 1,)), dma((n_src - 1,)),
            dma((core_n,)), dma((core_n,)), dma((x_n,)), dma((x_n,)), dma((z_n,)), dma((z_n,)),
            dma((z_n,)), dma((z_n,)), dma((x_n,)), dma((x_n,)), dma((core_n,)), dma((core_n,)),
        ],
        compiler_params=pltpu.CompilerParams(
            collective_id=1, has_side_effects=True, vmem_limit_bytes=LIMIT
        ),
        name="give_back",
    )(sgrad, tgrad, rgrad, source_lists, target_lists)

    new_source_table, new_source_state = update_rows(source_table, source_state, source_sum)
    new_target_table, new_target_state = update_rows(target_table, target_state, target_sum)
    new_relation_table, new_relation_state = update_rows(
        relation_table, relation_state, relation_total.astype(F32)
    )
    return (
        new_source_table, new_source_state, new_target_table, new_target_state,
        new_relation_table, new_relation_state,
    )


def solution(mesh):
    every = ("groups", "src", "dst")
    rows = P(every, None)
    flat = P(every)
    outs = (rows, flat, rows, flat, P("groups", None), P("groups"))
    return jax.shard_map(
        body,
        mesh=mesh,
        in_specs=outs + (P(None, every), flat, rows, rows, rows),
        out_specs=outs,
        check_vma=False,
    )
```

```python
import functools

import jax
import jax.numpy as jnp
from jax import lax
from jax.experimental import pallas as pl
from jax.experimental.pallas import tpu as pltpu
from jax.sharding import PartitionSpec as P

learn_rate = 0.1
MESH = pl.DeviceIdType.MESH
BF = jnp.bfloat16
F32 = jnp.float32


def dot(a, b):
    return jnp.dot(a, b, preferred_element_type=F32)


def dot_nt(a, b):
    return lax.dot_general(a, b, (((1,), (1,)), ((), ())), preferred_element_type=F32)


def dot_tn(a, b):
    return lax.dot_general(a, b, (((0,), (0,)), ((), ())), preferred_element_type=F32)


def one_hot(rows, ids):
    where = lax.broadcasted_iota(jnp.int32, (rows, ids.shape[1]), 0) == ids
    return jnp.where(where, 1.0, 0.0).astype(BF)


def greet(n_src, n_dst, me_s, me_d):
    barrier = pltpu.get_barrier_semaphore()
    for k in range(1, n_dst):
        pl.semaphore_signal(
            barrier, 1, device_id={"dst": lax.rem(me_d + k, n_dst)}, device_id_type=MESH
        )
    for k in range(1, n_src):
        pl.semaphore_signal(
            barrier, 1, device_id={"src": lax.rem(me_s + k, n_src)}, device_id_type=MESH
        )
    return barrier


def swap(axis, n, me, cap, out_ref, in_ref, send, recv):
    copies = []
    for k in range(1, n):
        peer = lax.rem(me + k, n)
        copy = pltpu.make_async_remote_copy(
            src_ref=out_ref.at[pl.ds(pl.multiple_of(peer * cap, cap), cap)],
            dst_ref=in_ref.at[pl.ds(pl.multiple_of(me * cap, cap), cap)],
            send_sem=send.at[k - 1],
            recv_sem=recv.at[k - 1],
            device_id={axis: peer},
            device_id_type=MESH,
        )
        copy.start()
        copies.append(copy)
    return copies


def row_of(lists):
    return jnp.concatenate([lists[p : p + 1, :] for p in range(lists.shape[0])], axis=1)


def step_kernel(
    n_src, n_dst, pieces, step,
    stab, ttab, rel, edges, count, negs, slist, tlist,
    ssum, tsum, total,
    sout, tout, sin, tin, sgrad, tgrad, sback, tback,
    relation_of, src_t, dst_t, hots, rg, packed,
    core_in, x_in, z_in, core_sum, x_sum, full,
    f1, f2, f3, f4, s1, r1, s2, r2,
    cs_s, cs_r, xs_s, xs_r, zs_s, zs_r, zg_s, zg_r, xg_s, xg_r, cg_s, cg_r,
):
    me_s = lax.axis_index("src")
    me_d = lax.axis_index("dst")
    core = lax.rem(me_d, 2)
    chip = me_d // 2
    chips = n_dst // 2
    other = me_d + 1 - 2 * core
    cs = slist.shape[1]
    cd = tlist.shape[1]
    own = stab.shape[1]
    slots = n_dst * cs
    targets = n_src * cd
    width, relations = rel.shape
    half = width // 2
    blocks, negatives = negs.shape
    span = edges.shape[1] // blocks
    z_rows = step
    x_rows = z_rows * n_src
    c_rows = x_rows * chips
    p_rows = c_rows * 2

    barrier = greet(n_src, n_dst, me_s, me_d)
    hot_target = one_hot(own, row_of(tlist))
    hot_source = one_hot(own, row_of(slist))
    tout[...] = dot(ttab[...].astype(BF), hot_target).astype(BF).T
    sout[...] = dot(stab[...].astype(BF), hot_source).astype(BF).T
    pl.semaphore_wait(barrier, n_src + n_dst - 2)
    second = swap("src", n_src, me_s, cd, tout, tin, f3, f4)
    first = swap("dst", n_dst, me_d, cs, sout, sin, f1, f2)
    mine_s = pl.ds(pl.multiple_of(me_d * cs, cs), cs)
    mine_d = pl.ds(pl.multiple_of(me_s * cd, cd), cd)
    sin[mine_s, :] = sout[mine_s, :]
    tin[mine_d, :] = tout[mine_d, :]

    table = rel[...]
    rel_high = table.astype(BF)
    rel_rest = (table - rel_high.astype(F32)).astype(BF)
    for c in range(blocks):
        cols = slice(c * span, (c + 1) * span)
        hot_r = one_hot(relations, edges[1:2, cols])
        hots[:, cols] = hot_r
        relation_of[:, cols] = dot(rel_high, hot_r) + dot(rel_rest, hot_r)

    for copy in second:
        copy.wait()
    for copy in first:
        copy.wait()
    src_t[...] = sin[...].T
    dst_t[...] = tin[...].T
    source_acc = jnp.zeros((slots, width), F32)
    target_acc = jnp.zeros((targets, width), F32)
    live = count[0]
    for c in range(blocks):
        cols = slice(c * span, (c + 1) * span)
        uses = one_hot(targets, negs[c : c + 1, :])
        uses = jnp.sum(uses.astype(F32), axis=1, keepdims=True)
        hot_s = one_hot(slots, edges[0:1, cols])
        is_target = (
            lax.broadcasted_iota(jnp.int32, (targets, span), 0) == edges[2:3, cols]
        )
        place = c * span + lax.broadcasted_iota(jnp.int32, (1, span), 1)
        alive = jnp.where(place < live, 1.0, 0.0)
        source = dot(src_t[...], hot_s)
        relation = relation_of[:, cols]
        sr, si = source[:half], source[half:]
        rr, ri = relation[:half], relation[half:]
        query = jnp.concatenate([sr * rr - si * ri, sr * ri + si * rr], axis=0)
        low = query.astype(BF)
        rest = (query - low.astype(F32)).astype(BF)
        logits = dot(tin[...], low)
        extra = dot(tin[...], rest)
        positive = jnp.sum(jnp.where(is_target, logits + extra, 0.0), axis=0, keepdims=True)
        pos_weight = -alive * jax.nn.sigmoid(-positive)
        neg_weight = (jax.nn.sigmoid(logits) * (alive / negatives)).astype(BF).astype(F32)
        weight = jnp.where(is_target, pos_weight, 0.0) + uses * neg_weight
        w_high = weight.astype(BF)
        w_rest = (weight - w_high.astype(F32)).astype(BF)
        grad = dot(dst_t[...], w_high) + dot(dst_t[...], w_rest)
        target_acc = target_acc + (
            dot_nt(w_high, low) + (dot_nt(w_rest, low) + dot_nt(w_high, rest))
        )
        gr, gi = grad[:half], grad[half:]
        source_grad = jnp.concatenate([gr * rr + gi * ri, gi * rr - gr * ri], axis=0)
        source_acc = source_acc + dot_nt(hot_s, source_grad.astype(BF))
        rg[:, cols] = jnp.concatenate(
            [gr * sr + gi * si, gi * sr - gr * si], axis=0
        ).astype(BF)

    def rows(start, count):
        return pl.ds(pl.multiple_of(start, 16), count)

    def push(src, dst, send, recv, axis, peer):
        copy = pltpu.make_async_remote_copy(
            src_ref=src, dst_ref=dst, send_sem=send, recv_sem=recv,
            device_id={axis: peer}, device_id_type=MESH,
        )
        copy.start()
        return copy

    started = {}

    def stage_core(p):
        started["c", p] = [
            push(
                packed.at[rows(p * p_rows + (1 - core) * c_rows, c_rows)],
                core_in.at[pl.ds(p * c_rows, c_rows)],
                cs_s.at[p], cs_r.at[p], "dst", other,
            )
        ]

    def stage_x(p):
        for copy in started["c", p]:
            copy.wait()
        here = pl.ds(p * c_rows, c_rows)
        own = packed[rows(p * p_rows + core * c_rows, c_rows), :]
        core_sum[here, :] = (own.astype(F32) + core_in[here, :].astype(F32)).astype(BF)
        started["x", p] = []
        for k in range(1, chips):
            peer = lax.rem(chip + k, chips)
            slot = p * (chips - 1) + k - 1
            started["x", p].append(
                push(
                    core_sum.at[rows(p * c_rows + peer * x_rows, x_rows)],
                    x_in.at[pl.ds(slot * x_rows, x_rows)],
                    xs_s.at[slot], xs_r.at[slot], "dst", peer * 2 + core,
                )
            )

    def stage_z(p):
        for copy in started["x", p]:
            copy.wait()
        value = core_sum[rows(p * c_rows + chip * x_rows, x_rows), :].astype(F32)
        for k in range(1, chips):
            slot = p * (chips - 1) + k - 1
            value = value + x_in[pl.ds(slot * x_rows, x_rows), :].astype(F32)
        x_sum[pl.ds(p * x_rows, x_rows), :] = value.astype(BF)
        started["z", p] = []
        for k in range(1, n_src):
            peer = lax.rem(me_s + k, n_src)
            slot = p * (n_src - 1) + k - 1
            started["z", p].append(
                push(
                    x_sum.at[rows(p * x_rows + peer * z_rows, z_rows)],
                    z_in.at[pl.ds(slot * z_rows, z_rows)],
                    zs_s.at[slot], zs_r.at[slot], "src", peer,
                )
            )

    def place(p, chip_at, src_at):
        return p * p_rows + core * c_rows + chip_at * x_rows + src_at * z_rows

    def gather_z(p):
        for copy in started["z", p]:
            copy.wait()
        value = x_sum[rows(p * x_rows + me_s * z_rows, z_rows), :].astype(F32)
        for k in range(1, n_src):
            slot = p * (n_src - 1) + k - 1
            value = value + z_in[pl.ds(slot * z_rows, z_rows), :].astype(F32)
        here = rows(place(p, chip, me_s), z_rows)
        full[here, :] = value.astype(BF)
        started["gz", p] = []
        for k in range(1, n_src):
            peer = lax.rem(me_s + k, n_src)
            slot = p * (n_src - 1) + k - 1
            started["gz", p].append(
                push(full.at[here], full.at[here], zg_s.at[slot], zg_r.at[slot], "src", peer)
            )

    def gather_x(p):
        for copy in started["gz", p]:
            copy.wait()
        here = rows(place(p, chip, 0), x_rows)
        started["gx", p] = []
        for k in range(1, chips):
            peer = lax.rem(chip + k, chips)
            slot = p * (chips - 1) + k - 1
            started["gx", p].append(
                push(
                    full.at[here], full.at[here], xg_s.at[slot], xg_r.at[slot],
                    "dst", peer * 2 + core,
                )
            )

    def gather_core(p):
        for copy in started["gx", p]:
            copy.wait()
        here = rows(place(p, 0, 0), c_rows)
        started["gc", p] = [
            push(full.at[here], full.at[here], cg_s.at[p], cg_r.at[p], "dst", other)
        ]

    def sums():
        for copy in back_s:
            copy.wait()
        ssum[...] = dot_nt(sback[...].T, hot_source)
        for copy in back_t:
            copy.wait()
        tsum[...] = dot_nt(tback[...].T, hot_target)

    used = (relations // 128) * width
    if packed.shape[0] > used:
        packed[used:, :] = jnp.zeros((packed.shape[0] - used, 128), BF)
    sent = 0
    for j in range(0, relations, 256):
        wide = min(256, relations - j)
        value = dot_nt(rg[...], hots[j : j + wide, :]).astype(BF)
        for i in range(0, wide, 128):
            at = ((j + i) // 128) * width
            packed[at : at + width, :] = value[:, i : i + 128]
        ready = ((j + wide) // 128) * width
        if j + wide == relations:
            ready = packed.shape[0]
        while sent < pieces and (sent + 1) * p_rows <= ready:
            stage_core(sent)
            if sent:
                stage_x(sent - 1)
            sent += 1
    stage_x(pieces - 1)
    sgrad[...] = source_acc.astype(BF)
    tgrad[...] = target_acc.astype(BF)
    back_s = swap("dst", n_dst, me_d, cs, sgrad, sback, s1, r1)
    back_t = swap("src", n_src, me_s, cd, tgrad, tback, s2, r2)
    sback[mine_s, :] = sgrad[mine_s, :]
    tback[mine_d, :] = tgrad[mine_d, :]
    for p in range(pieces):
        stage_z(p)
    for t in range(pieces + 2):
        if t < pieces:
            gather_z(t)
        if 0 <= t - 1 < pieces:
            gather_x(t - 1)
        if 0 <= t - 2 < pieces:
            gather_core(t - 2)
    sums()
    for p in range(pieces):
        for copy in started["gc", p]:
            copy.wait()
    total[...] = full[...]


def update_kernel(
    stab, sstate, ssum, ttab, tstate, tsum, rel, rstate, total,
    new_s, new_ss, new_t, new_ts, new_r, new_rs,
    out_s, out_t, out_r, sems,
):
    width, relations = rel.shape

    def update(table, state, grad):
        new_state = state + jnp.sum(grad * grad, axis=0, keepdims=True) / width
        return table - grad * (learn_rate / jnp.sqrt(new_state)), new_state

    copies = []

    def leave(src, dst):
        copy = pltpu.make_async_copy(src, dst, sems.at[len(copies)])
        copy.start()
        copies.append(copy)

    out_s[...], new_ss[...] = update(stab[...], sstate[...], ssum[...])
    leave(out_s, new_s)
    out_t[...], new_ts[...] = update(ttab[...], tstate[...], tsum[...])
    leave(out_t, new_t)
    for j in range(relations // 128):
        cols = slice(j * 128, (j + 1) * 128)
        out_r[:, cols], new_rs[:, cols] = update(
            rel[:, cols], rstate[:, cols], total[j * width : (j + 1) * width, :].astype(F32)
        )
        if j % 2 == 1 or j == relations // 128 - 1:
            done = slice((j - j % 2) * 128, (j + 1) * 128)
            leave(out_r.at[:, done], new_r.at[:, done])
    for copy in copies:
        copy.wait()


VM = pl.BlockSpec(memory_space=pltpu.VMEM)
SM = pl.BlockSpec(memory_space=pltpu.SMEM)
HB = pl.BlockSpec(memory_space=pl.ANY)
LIMIT = 48 * 1024 * 1024


def body(
    source_table, source_state, target_table, target_state, relation_table, relation_state,
    edge_list, edge_count, negative_ids, source_lists, target_lists,
):
    n_dst = lax.axis_size("dst")
    n_src = lax.axis_size("src")
    width = source_table.shape[1]
    cs = source_lists.shape[1]
    cd = target_lists.shape[1]
    own = source_table.shape[0]
    relations = relation_table.shape[0]
    edges = edge_list.shape[1]
    group = n_src * n_dst
    chips = n_dst // 2
    slots, targets = n_dst * cs, n_src * cd
    share = -(-(relations // 128) * width // (group * 16)) * 16
    step = 64 if share % 64 == 0 else share
    pieces = share // step
    padded = share * group
    x_rows = step * n_src
    c_rows = x_rows * chips
    x_n = pieces * (chips - 1)
    z_n = pieces * (n_src - 1)
    dma = pltpu.SemaphoreType.DMA
    flat_s, flat_t, flat_r = source_table.T, target_table.T, relation_table.T

    source_sum, target_sum, total = pl.pallas_call(
        functools.partial(step_kernel, n_src, n_dst, pieces, step),
        out_shape=[
            jax.ShapeDtypeStruct((width, own), F32),
            jax.ShapeDtypeStruct((width, own), F32),
            jax.ShapeDtypeStruct((padded, 128), BF),
        ],
        in_specs=[VM, VM, VM, VM, SM, VM, VM, VM],
        out_specs=[VM] * 3,
        scratch_shapes=[pltpu.VMEM((slots, width), BF), pltpu.VMEM((targets, width), BF)] * 4
        + [
            pltpu.VMEM((width, edges), F32),
            pltpu.VMEM((width, slots), BF),
            pltpu.VMEM((width, targets), BF),
            pltpu.VMEM((relations, edges), BF),
            pltpu.VMEM((width, edges), BF),
            pltpu.VMEM((padded, 128), BF),
            pltpu.VMEM((pieces * c_rows, 128), BF),
            pltpu.VMEM((x_n * x_rows, 128), BF),
            pltpu.VMEM((z_n * step, 128), BF),
            pltpu.VMEM((pieces * c_rows, 128), BF),
            pltpu.VMEM((pieces * x_rows, 128), BF),
            pltpu.VMEM((padded, 128), BF),
        ]
        + [dma((n_dst - 1,)), dma((n_dst - 1,)), dma((n_src - 1,)), dma((n_src - 1,))] * 2
        + [dma((n,)) for n in (pieces, pieces, x_n, x_n, z_n, z_n, z_n, z_n, x_n, x_n, pieces, pieces)],
        compiler_params=pltpu.CompilerParams(
            collective_id=0, has_side_effects=True, vmem_limit_bytes=LIMIT
        ),
        name="step",
    )(
        flat_s, flat_t, flat_r, edge_list, edge_count, negative_ids, source_lists, target_lists,
    )

    line = lambda n: jax.ShapeDtypeStruct((1, n), F32)
    new_s, new_ss, new_t, new_ts, new_r, new_rs = pl.pallas_call(
        update_kernel,
        out_shape=[
            jax.ShapeDtypeStruct((width, own), F32), line(own),
            jax.ShapeDtypeStruct((width, own), F32), line(own),
            jax.ShapeDtypeStruct((width, relations), F32), line(relations),
        ],
        in_specs=[VM] * 9,
        out_specs=[HB, VM] * 3,
        scratch_shapes=[
            pltpu.VMEM((width, own), F32),
            pltpu.VMEM((width, own), F32),
            pltpu.VMEM((width, relations), F32),
            dma((2 + (relations // 128 + 1) // 2,)),
        ],
        compiler_params=pltpu.CompilerParams(vmem_limit_bytes=LIMIT),
        name="update",
    )(
        flat_s, source_state[None], source_sum, flat_t, target_state[None], target_sum,
        flat_r, relation_state[None], total,
    )
    return (new_s.T, new_ss[0], new_t.T, new_ts[0], new_r.T, new_rs[0])


def solution(mesh):
    every = ("groups", "src", "dst")
    rows = P(every, None)
    flat = P(every)
    outs = (rows, flat, rows, flat, P("groups", None), P("groups"))
    return jax.shard_map(
        body,
        mesh=mesh,
        in_specs=outs + (P(None, every), flat, rows, rows, rows),
        out_specs=outs,
        check_vma=False,
    )
```

```python
import functools

import jax
import jax.numpy as jnp
from jax import lax
from jax.experimental import pallas as pl
from jax.experimental.pallas import tpu as pltpu
from jax.sharding import PartitionSpec as P

learn_rate = 0.1
MESH = pl.DeviceIdType.MESH
BF = jnp.bfloat16
F32 = jnp.float32


def dot(a, b):
    return jnp.dot(a, b, preferred_element_type=F32)


def dot_nt(a, b):
    return lax.dot_general(a, b, (((1,), (1,)), ((), ())), preferred_element_type=F32)


def dot_tn(a, b):
    return lax.dot_general(a, b, (((0,), (0,)), ((), ())), preferred_element_type=F32)


def one_hot(rows, ids):
    where = lax.broadcasted_iota(jnp.int32, (rows, ids.shape[1]), 0) == ids
    return jnp.where(where, 1.0, 0.0).astype(BF)


def greet(n_src, n_dst, me_s, me_d):
    barrier = pltpu.get_barrier_semaphore()
    for k in range(1, n_dst):
        pl.semaphore_signal(
            barrier, 1, device_id={"dst": lax.rem(me_d + k, n_dst)}, device_id_type=MESH
        )
    for k in range(1, n_src):
        pl.semaphore_signal(
            barrier, 1, device_id={"src": lax.rem(me_s + k, n_src)}, device_id_type=MESH
        )
    return barrier


def swap(axis, n, me, cap, out_ref, in_ref, send, recv):
    copies = []
    for k in range(1, n):
        peer = lax.rem(me + k, n)
        copy = pltpu.make_async_remote_copy(
            src_ref=out_ref.at[pl.ds(pl.multiple_of(peer * cap, cap), cap)],
            dst_ref=in_ref.at[pl.ds(pl.multiple_of(me * cap, cap), cap)],
            send_sem=send.at[k - 1],
            recv_sem=recv.at[k - 1],
            device_id={axis: peer},
            device_id_type=MESH,
        )
        copy.start()
        copies.append(copy)
    return copies


def row_of(lists):
    return jnp.concatenate([lists[p : p + 1, :] for p in range(lists.shape[0])], axis=1)


def step_kernel(
    n_src, n_dst, pieces, step,
    stab_at, ttab_at, rel_at, edges_at, count, negs_at, slist_at, tlist_at,
    ssum_at, tsum_at, total_at,
    ssum, tsum, out_sems, stab, ttab, rel, edges, negs, slist, tlist, in_sems,
    sout, tout, sin, tin, sgrad, tgrad, sback, tback,
    relation_of, src_t, dst_t, hots, rg, packed,
    core_in, x_in, z_in, core_sum, x_sum, full,
    f1, f2, f3, f4, s1, r1, s2, r2,
    cs_s, cs_r, xs_s, xs_r, zs_s, zs_r, zg_s, zg_r, xg_s, xg_r, cg_s, cg_r,
):
    me_s = lax.axis_index("src")
    me_d = lax.axis_index("dst")
    core = lax.rem(me_d, 2)
    chip = me_d // 2
    chips = n_dst // 2
    other = me_d + 1 - 2 * core
    cs = slist.shape[1]
    cd = tlist.shape[1]
    own = stab.shape[1]
    slots = n_dst * cs
    targets = n_src * cd
    width, relations = rel.shape
    half = width // 2
    blocks, negatives = negs.shape
    span = edges.shape[1] // blocks
    z_rows = step
    x_rows = z_rows * n_src
    c_rows = x_rows * chips
    p_rows = c_rows * 2

    loads = []
    for src, dst in (
        (tlist_at, tlist), (ttab_at, ttab), (slist_at, slist), (stab_at, stab),
        (edges_at, edges), (rel_at, rel), (negs_at, negs),
    ):
        load = pltpu.make_async_copy(src, dst, in_sems.at[len(loads)])
        load.start()
        loads.append(load)
    barrier = greet(n_src, n_dst, me_s, me_d)
    loads[0].wait()
    loads[1].wait()
    hot_target = one_hot(own, row_of(tlist))
    tout[...] = dot(ttab[...].astype(BF), hot_target).astype(BF).T
    loads[2].wait()
    loads[3].wait()
    hot_source = one_hot(own, row_of(slist))
    sout[...] = dot(stab[...].astype(BF), hot_source).astype(BF).T
    pl.semaphore_wait(barrier, n_src + n_dst - 2)
    second = swap("src", n_src, me_s, cd, tout, tin, f3, f4)
    first = swap("dst", n_dst, me_d, cs, sout, sin, f1, f2)
    mine_s = pl.ds(pl.multiple_of(me_d * cs, cs), cs)
    mine_d = pl.ds(pl.multiple_of(me_s * cd, cd), cd)
    sin[mine_s, :] = sout[mine_s, :]
    tin[mine_d, :] = tout[mine_d, :]

    for load in loads[4:]:
        load.wait()
    table = rel[...]
    rel_high = table.astype(BF)
    rel_rest = (table - rel_high.astype(F32)).astype(BF)
    for c in range(blocks):
        cols = slice(c * span, (c + 1) * span)
        hot_r = one_hot(relations, edges[1:2, cols])
        hots[:, cols] = hot_r
        relation_of[:, cols] = dot(rel_high, hot_r) + dot(rel_rest, hot_r)

    for copy in second:
        copy.wait()
    for copy in first:
        copy.wait()
    src_t[...] = sin[...].T
    dst_t[...] = tin[...].T
    source_acc = jnp.zeros((slots, width), F32)
    target_acc = jnp.zeros((targets, width), F32)
    live = count[0]
    for c in range(blocks):
        cols = slice(c * span, (c + 1) * span)
        uses = one_hot(targets, negs[c : c + 1, :])
        uses = jnp.sum(uses.astype(F32), axis=1, keepdims=True)
        hot_s = one_hot(slots, edges[0:1, cols])
        is_target = (
            lax.broadcasted_iota(jnp.int32, (targets, span), 0) == edges[2:3, cols]
        )
        place = c * span + lax.broadcasted_iota(jnp.int32, (1, span), 1)
        alive = jnp.where(place < live, 1.0, 0.0)
        source = dot(src_t[...], hot_s)
        relation = relation_of[:, cols]
        sr, si = source[:half], source[half:]
        rr, ri = relation[:half], relation[half:]
        query = jnp.concatenate([sr * rr - si * ri, sr * ri + si * rr], axis=0)
        low = query.astype(BF)
        rest = (query - low.astype(F32)).astype(BF)
        logits = dot(tin[...], low)
        extra = dot(tin[...], rest)
        positive = jnp.sum(jnp.where(is_target, logits + extra, 0.0), axis=0, keepdims=True)
        pos_weight = -alive * jax.nn.sigmoid(-positive)
        neg_weight = (jax.nn.sigmoid(logits) * (alive / negatives)).astype(BF).astype(F32)
        weight = jnp.where(is_target, pos_weight, 0.0) + uses * neg_weight
        w_high = weight.astype(BF)
        w_rest = (weight - w_high.astype(F32)).astype(BF)
        grad = dot(dst_t[...], w_high) + dot(dst_t[...], w_rest)
        target_acc = target_acc + (
            dot_nt(w_high, low) + (dot_nt(w_rest, low) + dot_nt(w_high, rest))
        )
        gr, gi = grad[:half], grad[half:]
        source_grad = jnp.concatenate([gr * rr + gi * ri, gi * rr - gr * ri], axis=0)
        source_acc = source_acc + dot_nt(hot_s, source_grad.astype(BF))
        rg[:, cols] = jnp.concatenate(
            [gr * sr + gi * si, gi * sr - gr * si], axis=0
        ).astype(BF)

    def rows(start, count):
        return pl.ds(pl.multiple_of(start, 16), count)

    def push(src, dst, send, recv, axis, peer):
        copy = pltpu.make_async_remote_copy(
            src_ref=src, dst_ref=dst, send_sem=send, recv_sem=recv,
            device_id={axis: peer}, device_id_type=MESH,
        )
        copy.start()
        return copy

    started = {}
    leaving = []

    def leave(src, dst):
        copy = pltpu.make_async_copy(src, dst, out_sems.at[len(leaving)])
        copy.start()
        leaving.append(copy)


    def stage_core(p):
        started["c", p] = [
            push(
                packed.at[rows(p * p_rows + (1 - core) * c_rows, c_rows)],
                core_in.at[pl.ds(p * c_rows, c_rows)],
                cs_s.at[p], cs_r.at[p], "dst", other,
            )
        ]

    def stage_x(p):
        for copy in started["c", p]:
            copy.wait()
        here = pl.ds(p * c_rows, c_rows)
        own = packed[rows(p * p_rows + core * c_rows, c_rows), :]
        core_sum[here, :] = (own.astype(F32) + core_in[here, :].astype(F32)).astype(BF)
        started["x", p] = []
        for k in range(1, chips):
            peer = lax.rem(chip + k, chips)
            slot = p * (chips - 1) + k - 1
            started["x", p].append(
                push(
                    core_sum.at[rows(p * c_rows + peer * x_rows, x_rows)],
                    x_in.at[pl.ds(slot * x_rows, x_rows)],
                    xs_s.at[slot], xs_r.at[slot], "dst", peer * 2 + core,
                )
            )

    def stage_z(p):
        for copy in started["x", p]:
            copy.wait()
        value = core_sum[rows(p * c_rows + chip * x_rows, x_rows), :].astype(F32)
        for k in range(1, chips):
            slot = p * (chips - 1) + k - 1
            value = value + x_in[pl.ds(slot * x_rows, x_rows), :].astype(F32)
        x_sum[pl.ds(p * x_rows, x_rows), :] = value.astype(BF)
        started["z", p] = []
        for k in range(1, n_src):
            peer = lax.rem(me_s + k, n_src)
            slot = p * (n_src - 1) + k - 1
            started["z", p].append(
                push(
                    x_sum.at[rows(p * x_rows + peer * z_rows, z_rows)],
                    z_in.at[pl.ds(slot * z_rows, z_rows)],
                    zs_s.at[slot], zs_r.at[slot], "src", peer,
                )
            )

    def place(p, chip_at, src_at):
        return p * p_rows + core * c_rows + chip_at * x_rows + src_at * z_rows

    def gather_z(p):
        for copy in started["z", p]:
            copy.wait()
        value = x_sum[rows(p * x_rows + me_s * z_rows, z_rows), :].astype(F32)
        for k in range(1, n_src):
            slot = p * (n_src - 1) + k - 1
            value = value + z_in[pl.ds(slot * z_rows, z_rows), :].astype(F32)
        here = rows(place(p, chip, me_s), z_rows)
        full[here, :] = value.astype(BF)
        started["gz", p] = []
        for k in range(1, n_src):
            peer = lax.rem(me_s + k, n_src)
            slot = p * (n_src - 1) + k - 1
            started["gz", p].append(
                push(full.at[here], full.at[here], zg_s.at[slot], zg_r.at[slot], "src", peer)
            )

    def gather_x(p):
        for copy in started["gz", p]:
            copy.wait()
        here = rows(place(p, chip, 0), x_rows)
        started["gx", p] = []
        for k in range(1, chips):
            peer = lax.rem(chip + k, chips)
            slot = p * (chips - 1) + k - 1
            started["gx", p].append(
                push(
                    full.at[here], full.at[here], xg_s.at[slot], xg_r.at[slot],
                    "dst", peer * 2 + core,
                )
            )

    def gather_core(p):
        for copy in started["gx", p]:
            copy.wait()
        here = rows(place(p, 0, 0), c_rows)
        started["gc", p] = [
            push(full.at[here], full.at[here], cg_s.at[p], cg_r.at[p], "dst", other)
        ]

    def sums():
        for copy in back_s:
            copy.wait()
        ssum[...] = dot_nt(sback[...].T, hot_source)
        leave(ssum, ssum_at)
        for copy in back_t:
            copy.wait()
        tsum[...] = dot_nt(tback[...].T, hot_target)
        leave(tsum, tsum_at)

    used = (relations // 128) * width
    if packed.shape[0] > used:
        packed[used:, :] = jnp.zeros((packed.shape[0] - used, 128), BF)
    sent = 0
    for j in range(0, relations, 256):
        wide = min(256, relations - j)
        value = dot_nt(rg[...], hots[j : j + wide, :]).astype(BF)
        for i in range(0, wide, 128):
            at = ((j + i) // 128) * width
            packed[at : at + width, :] = value[:, i : i + 128]
        ready = ((j + wide) // 128) * width
        if j + wide == relations:
            ready = packed.shape[0]
        while sent < pieces and (sent + 1) * p_rows <= ready:
            stage_core(sent)
            if sent:
                stage_x(sent - 1)
            sent += 1
    stage_x(pieces - 1)
    sgrad[...] = source_acc.astype(BF)
    tgrad[...] = target_acc.astype(BF)
    back_s = swap("dst", n_dst, me_d, cs, sgrad, sback, s1, r1)
    back_t = swap("src", n_src, me_s, cd, tgrad, tback, s2, r2)
    sback[mine_s, :] = sgrad[mine_s, :]
    tback[mine_d, :] = tgrad[mine_d, :]
    for p in range(pieces):
        stage_z(p)
    sums()
    for t in range(pieces + 2):
        if t < pieces:
            gather_z(t)
        if 0 <= t - 1 < pieces:
            gather_x(t - 1)
        if 0 <= t - 2 < pieces:
            gather_core(t - 2)
    for p in range(pieces):
        for copy in started["gc", p]:
            copy.wait()
        done = pl.ds(p * p_rows, p_rows)
        leave(full.at[done], total_at.at[done])
    for copy in leaving:
        copy.wait()


def update_kernel(
    stab, sstate, ssum, ttab, tstate, tsum, rel, rstate, total,
    new_s, new_ss, new_t, new_ts, new_r, new_rs,
    out_s, out_t, out_r, sems,
):
    width, relations = rel.shape

    def update(table, state, grad):
        new_state = state + jnp.sum(grad * grad, axis=0, keepdims=True) / width
        return table - grad * (learn_rate / jnp.sqrt(new_state)), new_state

    copies = []

    def leave(src, dst):
        copy = pltpu.make_async_copy(src, dst, sems.at[len(copies)])
        copy.start()
        copies.append(copy)

    out_s[...], state = update(stab[...], sstate[...][None], ssum[...])
    new_ss[...] = state[0]
    leave(out_s, new_s)
    out_t[...], state = update(ttab[...], tstate[...][None], tsum[...])
    new_ts[...] = state[0]
    leave(out_t, new_t)
    for j in range(relations // 128):
        cols = slice(j * 128, (j + 1) * 128)
        out_r[:, cols], state = update(
            rel[:, cols], rstate[cols][None], total[j * width : (j + 1) * width, :].astype(F32)
        )
        new_rs[cols] = state[0]
        if j % 2 == 1 or j == relations // 128 - 1:
            done = slice((j - j % 2) * 128, (j + 1) * 128)
            leave(out_r.at[:, done], new_r.at[:, done])
    for copy in copies:
        copy.wait()


VM = pl.BlockSpec(memory_space=pltpu.VMEM)
SM = pl.BlockSpec(memory_space=pltpu.SMEM)
HB = pl.BlockSpec(memory_space=pl.ANY)
LIMIT = 58 * 1024 * 1024


def body(
    source_table, source_state, target_table, target_state, relation_table, relation_state,
    edge_list, edge_count, negative_ids, source_lists, target_lists,
):
    n_dst = lax.axis_size("dst")
    n_src = lax.axis_size("src")
    width = source_table.shape[1]
    cs = source_lists.shape[1]
    cd = target_lists.shape[1]
    own = source_table.shape[0]
    relations = relation_table.shape[0]
    edges = edge_list.shape[1]
    group = n_src * n_dst
    chips = n_dst // 2
    slots, targets = n_dst * cs, n_src * cd
    share = -(-(relations // 128) * width // (group * 16)) * 16
    step = 128 if share % 128 == 0 else share
    pieces = share // step
    padded = share * group
    x_rows = step * n_src
    c_rows = x_rows * chips
    x_n = pieces * (chips - 1)
    z_n = pieces * (n_src - 1)
    dma = pltpu.SemaphoreType.DMA
    flat_s, flat_t, flat_r = source_table.T, target_table.T, relation_table.T

    source_sum, target_sum, total = pl.pallas_call(
        functools.partial(step_kernel, n_src, n_dst, pieces, step),
        out_shape=[
            jax.ShapeDtypeStruct((width, own), F32),
            jax.ShapeDtypeStruct((width, own), F32),
            jax.ShapeDtypeStruct((padded, 128), BF),
        ],
        in_specs=[HB, HB, HB, HB, SM, HB, HB, HB],
        out_specs=[HB] * 3,
        scratch_shapes=[
            pltpu.VMEM((width, own), F32),
            pltpu.VMEM((width, own), F32),
            dma((2 + pieces,)),
        ]
        + [
            pltpu.VMEM(x.shape, x.dtype)
            for x in (
                flat_s, flat_t, flat_r, edge_list, negative_ids, source_lists, target_lists
            )
        ]
        + [dma((7,))]
        + [pltpu.VMEM((slots, width), BF), pltpu.VMEM((targets, width), BF)] * 4
        + [
            pltpu.VMEM((width, edges), F32),
            pltpu.VMEM((width, slots), BF),
            pltpu.VMEM((width, targets), BF),
            pltpu.VMEM((relations, edges), BF),
            pltpu.VMEM((width, edges), BF),
            pltpu.VMEM((padded, 128), BF),
            pltpu.VMEM((pieces * c_rows, 128), BF),
            pltpu.VMEM((x_n * x_rows, 128), BF),
            pltpu.VMEM((z_n * step, 128), BF),
            pltpu.VMEM((pieces * c_rows, 128), BF),
            pltpu.VMEM((pieces * x_rows, 128), BF),
            pltpu.VMEM((padded, 128), BF),
        ]
        + [dma((n_dst - 1,)), dma((n_dst - 1,)), dma((n_src - 1,)), dma((n_src - 1,))] * 2
        + [dma((n,)) for n in (pieces, pieces, x_n, x_n, z_n, z_n, z_n, z_n, x_n, x_n, pieces, pieces)],
        compiler_params=pltpu.CompilerParams(
            collective_id=0, has_side_effects=True, vmem_limit_bytes=LIMIT
        ),
        name="step",
    )(
        flat_s, flat_t, flat_r, edge_list, edge_count, negative_ids, source_lists, target_lists,
    )

    line = lambda n: jax.ShapeDtypeStruct((n,), F32)
    new_s, new_ss, new_t, new_ts, new_r, new_rs = pl.pallas_call(
        update_kernel,
        out_shape=[
            jax.ShapeDtypeStruct((width, own), F32), line(own),
            jax.ShapeDtypeStruct((width, own), F32), line(own),
            jax.ShapeDtypeStruct((width, relations), F32), line(relations),
        ],
        in_specs=[VM] * 9,
        out_specs=[HB, VM] * 3,
        scratch_shapes=[
            pltpu.VMEM((width, own), F32),
            pltpu.VMEM((width, own), F32),
            pltpu.VMEM((width, relations), F32),
            dma((2 + (relations // 128 + 1) // 2,)),
        ],
        compiler_params=pltpu.CompilerParams(vmem_limit_bytes=LIMIT),
        name="update",
    )(
        flat_s, source_state, source_sum, flat_t, target_state, target_sum,
        flat_r, relation_state, total,
    )
    return (new_s.T, new_ss, new_t.T, new_ts, new_r.T, new_rs)


def solution(mesh):
    every = ("groups", "src", "dst")
    rows = P(every, None)
    flat = P(every)
    outs = (rows, flat, rows, flat, P("groups", None), P("groups"))
    return jax.shard_map(
        body,
        mesh=mesh,
        in_specs=outs + (P(None, every), flat, rows, rows, rows),
        out_specs=outs,
        check_vma=False,
    )
```
